512 devices in a mesh: raster: 32 (over x, y), slit: 16 (over z, core).
Axes of the slice: x: 4, y: 8, z: 8, core: 2. Of those that a mesh axis runs over, the one named last changes fastest.
Arguments:
- spectra: float32 [1048576, 512], P(('raster', 'slit')), as said below
- start: float32 [512, 64], replicated, may hold values from -0.25 to 0.25
Outputs:
- coefficients: float32 [1048576, 64], P(('raster', 'slit'))
The draws below stay inside these ranges and needn't reach their ends.
Inputs may be any that keep to these rules, and one draw needn't show every extreme that they name: `spectra`: every spectrum is a real-valued row of order one; the columns of every device's block are linearly independent.
All inputs are finite; a program needn't handle non-finite values.
Results may differ from the reference program's by a relative error of at most 0.0003.
Values sent between devices are 32-bit elements; how exact they have to be, the bound alone decides.
No kernel may reach another device: no remote copies, remote signals or barrier semaphores. Data moves between devices by JAX's collectives and lax.ppermute only.
A program may use at most 128 MiB of HBM per device.

```python
import math
import jax
import jax.numpy as jnp
from jax import lax

W = 512
K = 64
ITERS = 6
SPECTRA = 1048576


def draw_spectra(key, part):
    key = jax.random.fold_in(key, 1)
    key_perm, key_sign, key_coef, key_row = jax.random.split(key, 4)
    chosen = jax.random.permutation(key_perm, W).astype(jnp.float32)[:, None]
    wave = jnp.arange(W, dtype=jnp.float32)[None, :]
    weight_norm = jnp.where(chosen == 0.0, math.sqrt(1.0 / W), math.sqrt(2.0 / W))
    profiles = weight_norm * jnp.cos(math.pi * (wave + 0.5) * chosen / W)
    signs = jnp.where(jax.random.bernoulli(key_sign, 0.5, (1, W)), 1.0, -1.0).astype(jnp.float32)
    profiles = profiles * signs
    rank = jnp.arange(W, dtype=jnp.float32)
    leading = jnp.exp(math.log(0.6) * rank / (K - 1))
    trailing = 0.45 * jnp.exp(math.log(0.1 / 0.45) * (rank - K) / (W - K - 1))
    amplitude = jnp.where(rank < K, leading, trailing)[None, :]
    coef = jax.random.normal(key_coef, (SPECTRA, W), jnp.float32)
    row_scale = jnp.exp(jax.random.uniform(key_row, (SPECTRA, 1), jnp.float32, -0.55, 0.55))
    values = jnp.dot(coef * amplitude, profiles, precision=lax.Precision.HIGHEST, preferred_element_type=jnp.float32)
    return (values * row_scale).astype(jnp.float32)


def scatter_about(own_key, shape, spread, limit, kind=jnp.bfloat16):
    return jnp.clip(spread * jax.random.normal(own_key, shape, jnp.float32), -limit, limit).astype(kind)


def setup_inputs(seed: int = 0) -> dict:
    arg_keys = jax.random.split(jax.random.key(seed), 3)
    spectra = draw_spectra(jax.random.fold_in(arg_keys[2], 71), 0)
    start = scatter_about(arg_keys[1], (W, K), W ** -0.5, 0.25, jnp.float32)
    return dict(spectra=spectra, start=start)


def orthonormal(image):
    cross = jnp.dot(image.T.astype(jnp.float32), image.astype(jnp.float32), precision=lax.Precision.HIGHEST, preferred_element_type=jnp.float32)
    lower = jnp.linalg.cholesky(cross)
    return lax.linalg.triangular_solve(lower, image, left_side=False, lower=True, transpose_a=True)

def reference(spectra, start):
    gram = jnp.dot(spectra.T.astype(jnp.float32), spectra.astype(jnp.float32), precision=lax.Precision.HIGHEST, preferred_element_type=jnp.float32)
    upper = jnp.linalg.cholesky(gram).T
    basis = start
    for step in range(ITERS):
        inner = jnp.dot(upper.astype(jnp.float32), basis.astype(jnp.float32), precision=lax.Precision.HIGHEST, preferred_element_type=jnp.float32)
        image = jnp.dot(upper.T.astype(jnp.float32), inner.astype(jnp.float32), precision=lax.Precision.HIGHEST, preferred_element_type=jnp.float32)
        basis = orthonormal(image)
    return jnp.dot(spectra.astype(jnp.float32), basis.astype(jnp.float32), precision=lax.Precision.HIGHEST, preferred_element_type=jnp.float32)
```

```python
import functools

import jax
import jax.numpy as jnp
from jax import lax
from jax.experimental import pallas as pl
from jax.experimental.pallas import tpu as pltpu
from jax.sharding import Mesh, PartitionSpec as P

W = 512
K = 64
ITERS = 6
CHUNK = 256
HALF = 6 * 128
F32 = jnp.float32
BF16 = jnp.bfloat16
NN = (((1,), (0,)), ((), ()))
NT = (((1,), (1,)), ((), ()))
TN = (((0,), (0,)), ((), ()))


def mul(a, b, dims):
    return lax.dot_general(a, b, dims, preferred_element_type=F32)


def split(value):
    high = value.astype(BF16)
    return high, (value - high.astype(F32)).astype(BF16)


def gram_kernel(core_ref, spectra_ref, keep_ref, send_ref, acc):
    step = pl.program_id(0)

    @pl.when(step == 0)
    def _():
        acc[...] = jnp.zeros_like(acc)

    high, low = split(spectra_ref[...])
    h0, h1 = high[:, :256], high[:, 256:]
    l0, l1 = low[:, :256], low[:, 256:]
    acc[0] += 0.5 * mul(h0, h0, TN) + mul(h0, l0, TN)
    acc[1] += mul(h0, h1, TN) + mul(h0, l1, TN) + mul(l0, h1, TN)
    acc[2] += 0.5 * mul(h1, h1, TN) + mul(h1, l1, TN)

    @pl.when(step == pl.num_programs(0) - 1)
    def _():
        core = core_ref[0]
        for ref, half in ((keep_ref, core), (send_ref, 1 - core)):
            rows = pl.ds(pl.multiple_of(half * 128, 128), 128)
            for block in range(3):
                for side in range(2):
                    at = (2 * block + side) * 128
                    ref[at : at + 128, :] = acc[block, rows, side * 128 : side * 128 + 128]


def gram_halves(core, spectra):
    rows = spectra.shape[0]
    half = jax.ShapeDtypeStruct((HALF, 128), F32)
    whole = pl.BlockSpec((HALF, 128), lambda i: (0, 0))
    return pl.pallas_call(
        gram_kernel,
        grid=(rows // CHUNK,),
        in_specs=[
            pl.BlockSpec(memory_space=pltpu.SMEM),
            pl.BlockSpec((CHUNK, W), lambda i: (i, 0)),
        ],
        out_specs=[whole, whole],
        out_shape=[half, half],
        scratch_shapes=[pltpu.VMEM((3, 256, 256), F32)],
        compiler_params=pltpu.CompilerParams(vmem_limit_bytes=32 * 1024 * 1024),
    )(core, spectra)


def splat(value, i, j):
    return jnp.broadcast_to(value[i : i + 1, j : j + 1], (8, 128))


def eliminate(a, out_ref):
    for b in range(8):
        pivot = a[b]
        lane = 64 + 8 * b
        d = {(i, j): splat(pivot, i, lane + j) for i in range(8) for j in range(i + 1)}
        inv = []
        x = {}
        for k in range(8):
            inv.append(1.0 / d[k, k])
            m = {i: d[i, k] * inv[k] for i in range(k + 1, 8)}
            for i in range(k + 1, 8):
                for j in range(k + 1, i + 1):
                    d[i, j] = d[i, j] - (d[i, k] * d[j, k]) * inv[k]
                for j in range(k):
                    x[i, j] = x[i, j] - m[i] * x[k, j]
                x[i, k] = -m[i]
        rows = [jnp.broadcast_to(pivot[j : j + 1, :], (8, 128)) for j in range(8)]
        new = []
        for r in range(8):
            total = rows[r]
            for j in range(r):
                total = total + x[r, j] * rows[j]
            new.append(total)
        for r in range(8):
            out_ref[8 * b + r : 8 * b + r + 1, :] = (new[r] * lax.rsqrt(d[r, r]))[0:1, :]
        if b == 7:
            break
        scaled = [new[r] * inv[r] for r in range(8)]
        q = []
        for c in range(8):
            total = scaled[c]
            for j in range(c + 1, 8):
                total = total + x[j, c] * scaled[j]
            q.append(total)
        for i in range(b + 1, 8):
            total = a[i]
            for c in range(8):
                total = total - jnp.broadcast_to(a[i][:, lane + c : lane + c + 1], (8, 128)) * q[c]
            a[i] = total


def iterate_kernel(core_ref, mine_ref, other_ref, start_ref, spectra_ref, out_ref, gh, gl, basis, rp, sbuf, obuf, sem, osem):
    load = pltpu.make_async_copy(spectra_ref, sbuf, sem)
    load.start()
    core = core_ref[0]
    zero_is_mine = core == 0

    def half(h, block):
        at = slice(block * 128, block * 128 + 128)
        a, b = mine_ref[at, :], other_ref[at, :]
        return jnp.where(zero_is_mine, a, b) if h == 0 else jnp.where(zero_is_mine, b, a)

    def whole(block):
        return jnp.concatenate(
            [jnp.concatenate([half(h, 2 * block), half(h, 2 * block + 1)], axis=1) for h in range(2)], axis=0
        )

    def put(i, j, value):
        at = (slice(256 * i, 256 * i + 256), slice(256 * j, 256 * j + 256))
        gh[at], gl[at] = split(value * 2.0**-20)

    t0, t1, t2 = whole(0), whole(1), whole(2)
    put(0, 0, t0 + t0.T)
    put(0, 1, t1)
    put(1, 0, t1.T)
    put(1, 1, t2 + t2.T)

    basis[...] = start_ref[...].T
    lanes = lax.broadcasted_iota(jnp.int32, (K, 128), 1)
    eye = (lanes == lax.broadcasted_iota(jnp.int32, (K, 128), 0)).astype(F32)

    def step(_, carry):
        bh, bl = split(basis[...])
        both = mul(jnp.concatenate([bh, bl], axis=0), gh[...], NN)
        image = both[:K] + both[K:] + mul(bh, gl[...], NN)
        ih, il = split(image)
        first = mul(jnp.concatenate([ih, il], axis=0), jnp.concatenate([il, ih], axis=0), NT)
        cross = first[:K] + first[K:] + mul(ih, jnp.concatenate([ih, il], axis=0), NT)
        a = jnp.where(lanes < K, eye, cross)
        eliminate([a[8 * i : 8 * i + 8, :] for i in range(8)], rp)
        xh, xl = split(rp[:, :K])
        both = mul(jnp.concatenate([xh, xl], axis=0), ih, NN)
        basis[...] = both[:K] + both[K:] + mul(xh, il, NN)
        return carry

    lax.fori_loop(0, ITERS, step, 0)
    bh, bl = split(basis[...])
    load.wait()
    rows = 512
    both = jnp.concatenate([bh, bl], axis=0)

    @pl.loop(0, sbuf.shape[0] // rows)
    def _(i):
        at = pl.ds(pl.multiple_of(i * rows, rows), rows)
        sh, sl = split(sbuf[at, :])
        wide = mul(sh, both, NT)
        obuf[at, :] = wide[:, :K] + wide[:, K:] + mul(sl, bh, NT)

    store = pltpu.make_async_copy(obuf, out_ref, osem)
    store.start()
    store.wait()


def finish(core, mine, other, start, spectra):
    rows = spectra.shape[0]
    vmem = pl.BlockSpec(memory_space=pltpu.VMEM)
    hbm = pl.BlockSpec(memory_space=pl.ANY)
    return pl.pallas_call(
        iterate_kernel,
        in_specs=[pl.BlockSpec(memory_space=pltpu.SMEM), vmem, vmem, vmem, hbm],
        out_specs=hbm,
        out_shape=jax.ShapeDtypeStruct((rows, K), F32),
        scratch_shapes=[
            pltpu.VMEM((W, W), BF16),
            pltpu.VMEM((W, W), BF16),
            pltpu.VMEM((K, W), F32),
            pltpu.VMEM((K, 128), F32),
            pltpu.VMEM((rows, W), F32),
            pltpu.VMEM((rows, K), F32),
            pltpu.SemaphoreType.DMA,
            pltpu.SemaphoreType.DMA,
        ],
        compiler_params=pltpu.CompilerParams(vmem_limit_bytes=48 * 1024 * 1024),
    )(core, mine, other, start, spectra)


def swap(value):
    return lax.ppermute(value, "core", [(0, 1), (1, 0)])


def spread(piece, axis, copies):
    return lax.all_to_all(jnp.broadcast_to(piece[None], (copies, *piece.shape)), axis, 0, 0)


def body(raster, z, spectra, start):
    core = lax.axis_index("core").astype(jnp.int32).reshape(1)
    keep, send = gram_halves(core, spectra)
    part = keep + swap(send)
    part = lax.all_to_all(part.reshape(raster, HALF // raster, 128), "raster", 0, 0)
    piece = jnp.sum(part, axis=0)
    piece = jnp.sum(spread(piece, "z", z), axis=0)
    mine = spread(piece, "raster", raster).reshape(HALF, 128)
    return finish(core, mine, swap(mine), start, spectra)


def solution(mesh):
    raster, slit = mesh.devices.shape
    inner = Mesh(mesh.devices.reshape(raster, slit // 2, 2), ("raster", "z", "core"))
    rows = P(("raster", "z", "core"), None)
    return jax.shard_map(
        functools.partial(body, raster, slit // 2),
        mesh=inner,
        in_specs=(rows, P()),
        out_specs=rows,
        check_vma=False,
    )
```

```python
import functools

import jax
import jax.numpy as jnp
from jax import lax
from jax.experimental import pallas as pl
from jax.experimental.pallas import tpu as pltpu
from jax.sharding import Mesh, PartitionSpec as P

W = 512
K = 64
ITERS = 6
CHUNK = 512
HALF = 6 * 128
F32 = jnp.float32
BF16 = jnp.bfloat16
NN = (((1,), (0,)), ((), ()))
NT = (((1,), (1,)), ((), ()))
TN = (((0,), (0,)), ((), ()))


def mul(a, b, dims):
    return lax.dot_general(a, b, dims, preferred_element_type=F32)


def split(value):
    high = value.astype(BF16)
    return high, (value - high.astype(F32)).astype(BF16)


def gram_kernel(core_ref, spectra_ref, keep_ref, send_ref, buf, acc, sems):
    parts = buf.shape[0] // CHUNK
    loads = []
    for i in range(parts):
        at = slice(i * CHUNK, i * CHUNK + CHUNK)
        loads.append(pltpu.make_async_copy(spectra_ref.at[at], buf.at[at], sems.at[i]))
        loads[-1].start()
    for i in range(parts):
        loads[i].wait()
        high, low = split(buf[i * CHUNK : i * CHUNK + CHUNK, :])
        h0, h1 = high[:, :256], high[:, 256:]
        l0, l1 = low[:, :256], low[:, 256:]
        sums = (
            0.5 * mul(h0, h0, TN) + mul(h0, l0, TN),
            mul(h0, h1, TN) + mul(h0, l1, TN) + mul(l0, h1, TN),
            0.5 * mul(h1, h1, TN) + mul(h1, l1, TN),
        )
        for block in range(3):
            acc[block] = acc[block] + sums[block] if i else sums[block]
    for ref, half in ((keep_ref, core_ref[0]), (send_ref, 1 - core_ref[0])):
        rows = pl.ds(pl.multiple_of(half * 128, 128), 128)
        for block in range(3):
            for side in range(2):
                at = (2 * block + side) * 128
                ref[at : at + 128, :] = acc[block, rows, side * 128 : side * 128 + 128]


def gram_halves(core, spectra):
    rows = spectra.shape[0]
    half = jax.ShapeDtypeStruct((HALF, 128), F32)
    vmem = pl.BlockSpec(memory_space=pltpu.VMEM)
    return pl.pallas_call(
        gram_kernel,
        in_specs=[pl.BlockSpec(memory_space=pltpu.SMEM), pl.BlockSpec(memory_space=pl.ANY)],
        out_specs=[vmem, vmem],
        out_shape=[half, half],
        scratch_shapes=[
            pltpu.VMEM((rows, W), F32),
            pltpu.VMEM((3, 256, 256), F32),
            pltpu.SemaphoreType.DMA((rows // CHUNK,)),
        ],
        compiler_params=pltpu.CompilerParams(vmem_limit_bytes=52 * 1024 * 1024),
    )(core, spectra)


def tree(terms):
    while len(terms) > 1:
        terms = [terms[i] + terms[i + 1] if i + 1 < len(terms) else terms[i] for i in range(0, len(terms), 2)]
    return terms[0]


def lanes_of(group, lane):
    return jnp.broadcast_to(group[:, lane : lane + 1], (8, 128))


def row_of(group, i):
    return jnp.broadcast_to(group[i : i + 1, :], (8, 128))


def eliminate(a, out_ref):
    sub = lax.broadcasted_iota(jnp.int32, (8, 128), 0)
    square = [lanes_of(a[0], 64 + j) for j in range(8)]
    for b in range(8):
        lane = 64 + 8 * b
        nearest = [lanes_of(a[b + 1], lane + j) for j in range(8)] if b < 7 else []
        following = [lanes_of(a[b + 1], lane + 8 + j) for j in range(8)] if b < 7 else []
        rows = a[b]
        scaled = []
        inverse = jnp.zeros((8, 128), F32)
        for k in range(8):
            s = {c: row_of(square[k], c) for c in range(k, 8)}
            inv = pl.reciprocal(s[k], approx=True)
            below = jnp.where(sub > k, square[k], 0.0)
            down = below * inv
            for c in range(k + 1, 8):
                square[c] = square[c] - ((below * s[c]) * inv if c == k + 1 else down * s[c])
            row = row_of(rows, k)
            rows = rows - down * row
            inverse = jnp.where(sub == k, inv, inverse)
            if b < 7:
                scaled.append(row * inv)
                down = nearest[k] * inv
                for c in range(k + 1, 8):
                    nearest[c] = nearest[c] - down * s[c]
                for c in range(8):
                    following[c] = following[c] - down * row_of(nearest[k], c)
        out_ref[8 * b : 8 * b + 8, :] = rows * (inverse * lax.rsqrt(inverse))
        if b == 7:
            break
        a[b + 1] = a[b + 1] - tree([nearest[k] * scaled[k] for k in range(8)])
        panels = {i: [lanes_of(a[i], lane + j) for j in range(8)] for i in range(b + 2, 8)}
        if panels:
            q = rows * inverse
            for k in range(7, 0, -1):
                q = q - jnp.where(sub < k, square[k] * inverse, 0.0) * row_of(q, k)
            q = [row_of(q, c) for c in range(8)]
            for i, panel in panels.items():
                a[i] = a[i] - tree([panel[c] * q[c] for c in range(8)])
        square = following


def iterate_kernel(core_ref, mine_ref, other_ref, start_ref, spectra_ref, out_ref, gh, gl, basis, rp, sbuf, obuf, sem, osem):
    load = pltpu.make_async_copy(spectra_ref, sbuf, sem)
    load.start()
    core = core_ref[0]
    zero_is_mine = core == 0

    def half(h, block):
        at = slice(block * 128, block * 128 + 128)
        a, b = mine_ref[at, :], other_ref[at, :]
        return jnp.where(zero_is_mine, a, b) if h == 0 else jnp.where(zero_is_mine, b, a)

    def whole(block):
        return jnp.concatenate(
            [jnp.concatenate([half(h, 2 * block), half(h, 2 * block + 1)], axis=1) for h in range(2)], axis=0
        )

    def put(i, j, value):
        at = (slice(256 * i, 256 * i + 256), slice(256 * j, 256 * j + 256))
        gh[at], gl[at] = split(value * 2.0**-20)

    t0, t1, t2 = whole(0), whole(1), whole(2)
    put(0, 0, t0 + t0.T)
    put(0, 1, t1)
    put(1, 0, t1.T)
    put(1, 1, t2 + t2.T)

    basis[...] = start_ref[...]
    lanes = lax.broadcasted_iota(jnp.int32, (K, 128), 1)
    eye = (lanes == lax.broadcasted_iota(jnp.int32, (K, 128), 0)).astype(F32)

    def step(_, carry):
        bh, bl = split(basis[...])
        both = mul(jnp.concatenate([bh, bl], axis=0), gh[...], NN)
        image = both[:K] + both[K:] + mul(bh, gl[...], NN)
        ih, il = split(image)
        first = mul(jnp.concatenate([ih, il], axis=0), jnp.concatenate([il, ih], axis=0), NT)
        cross = first[:K] + first[K:] + mul(ih, jnp.concatenate([ih, il], axis=0), NT)
        a = jnp.where(lanes < K, eye, cross)
        eliminate([a[8 * i : 8 * i + 8, :] for i in range(8)], rp)
        xh, xl = split(rp[:, :K])
        both = mul(jnp.concatenate([xh, xl], axis=0), ih, NN)
        basis[...] = both[:K] + both[K:] + mul(xh, il, NN)
        return carry

    lax.fori_loop(0, ITERS, step, 0)
    bh, bl = split(basis[...])
    load.wait()
    both = jnp.concatenate([bh, bl], axis=0)
    rows = 512
    stores = []
    for i in range(sbuf.shape[0] // rows):
        at = slice(i * rows, i * rows + rows)
        sh, sl = split(sbuf[at, :])
        wide = mul(both, sh, NT)
        obuf[:, at] = wide[:K] + wide[K:] + mul(bh, sl, NT)
        stores.append(pltpu.make_async_copy(obuf.at[:, at], out_ref.at[:, at], osem.at[i]))
        stores[-1].start()
    for store in stores:
        store.wait()


def finish(core, mine, other, start, spectra):
    rows = spectra.shape[0]
    vmem = pl.BlockSpec(memory_space=pltpu.VMEM)
    hbm = pl.BlockSpec(memory_space=pl.ANY)
    return pl.pallas_call(
        iterate_kernel,
        in_specs=[pl.BlockSpec(memory_space=pltpu.SMEM), vmem, vmem, vmem, hbm],
        out_specs=hbm,
        out_shape=jax.ShapeDtypeStruct((K, rows), F32),
        scratch_shapes=[
            pltpu.VMEM((W, W), BF16),
            pltpu.VMEM((W, W), BF16),
            pltpu.VMEM((K, W), F32),
            pltpu.VMEM((K, 128), F32),
            pltpu.VMEM((rows, W), F32),
            pltpu.VMEM((K, rows), F32),
            pltpu.SemaphoreType.DMA,
            pltpu.SemaphoreType.DMA((rows // 512,)),
        ],
        compiler_params=pltpu.CompilerParams(vmem_limit_bytes=52 * 1024 * 1024),
    )(core, mine, other, start, spectra)


def swap(value):
    return lax.ppermute(value, "core", [(0, 1), (1, 0)])


def spread(piece, axis, copies):
    return lax.all_to_all(jnp.broadcast_to(piece[None], (copies, *piece.shape)), axis, 0, 0)


def body(raster, z, spectra, start):
    core = lax.axis_index("core").astype(jnp.int32).reshape(1)
    keep, send = gram_halves(core, spectra)
    part = keep + swap(send)
    part = lax.all_to_all(part.reshape(raster, HALF // raster, 128), "raster", 0, 0)
    piece = jnp.sum(part, axis=0)
    piece = jnp.sum(spread(piece, "z", z), axis=0)
    mine = spread(piece, "raster", raster).reshape(HALF, 128)
    return finish(core, mine, swap(mine), start.T, spectra).T


def solution(mesh):
    raster, slit = mesh.devices.shape
    inner = Mesh(mesh.devices.reshape(raster, slit // 2, 2), ("raster", "z", "core"))
    rows = P(("raster", "z", "core"), None)
    return jax.shard_map(
        functools.partial(body, raster, slit // 2),
        mesh=inner,
        in_specs=(rows, P()),
        out_specs=rows,
        check_vma=False,
    )
```

```python
import functools

import jax
import jax.numpy as jnp
from jax import lax
from jax.experimental import pallas as pl
from jax.experimental.pallas import tpu as pltpu
from jax.sharding import Mesh, PartitionSpec as P

W = 512
K = 64
ITERS = 6
CHUNK = 512
HALF = 5 * 128
BLOCKS = (((0, 0), (0, 1), (0, 2), (0, 3), (3, 3)), ((1, 1), (1, 2), (1, 3), (2, 2), (2, 3)))
F32 = jnp.float32
BF16 = jnp.bfloat16
NN = (((1,), (0,)), ((), ()))
NT = (((1,), (1,)), ((), ()))
TN = (((0,), (0,)), ((), ()))


def mul(a, b, dims):
    return lax.dot_general(a, b, dims, preferred_element_type=F32)


def split(value):
    high = value.astype(BF16)
    return high, (value - high.astype(F32)).astype(BF16)


def gram_kernel(core_ref, spectra_ref, keep_ref, send_ref, buf, acc, sems):
    parts = buf.shape[0] // CHUNK
    loads = []
    for i in range(parts):
        at = slice(i * CHUNK, i * CHUNK + CHUNK)
        loads.append(pltpu.make_async_copy(spectra_ref.at[at], buf.at[at], sems.at[i]))
        loads[-1].start()
    for i in range(parts):
        loads[i].wait()
        high, low = split(buf[i * CHUNK : i * CHUNK + CHUNK, :])
        h0, h1 = high[:, :256], high[:, 256:]
        l0, l1 = low[:, :256], low[:, 256:]
        sums = (
            0.5 * mul(h0, h0, TN) + mul(h0, l0, TN),
            mul(h0, h1, TN) + mul(h0, l1, TN) + mul(l0, h1, TN),
            0.5 * mul(h1, h1, TN) + mul(h1, l1, TN),
        )
        for block in range(3):
            acc[block] = acc[block] + sums[block] if i else sums[block]

    def block(i, j):
        rows, columns = i % 2 * 128, j % 2 * 128
        return acc[i // 2 + j // 2, rows : rows + 128, columns : columns + 128]

    def put(ref, half):
        for n, (i, j) in enumerate(BLOCKS[half]):
            value = block(i, j)
            if i != j and i // 2 == j // 2:
                value = value + block(j, i).T
            ref[n * 128 : n * 128 + 128, :] = value

    for core in range(2):

        @pl.when(core_ref[0] == core)
        def _():
            put(keep_ref, core)
            put(send_ref, 1 - core)


def gram_halves(core, spectra):
    rows = spectra.shape[0]
    half = jax.ShapeDtypeStruct((HALF, 128), F32)
    vmem = pl.BlockSpec(memory_space=pltpu.VMEM)
    return pl.pallas_call(
        gram_kernel,
        in_specs=[pl.BlockSpec(memory_space=pltpu.SMEM), pl.BlockSpec(memory_space=pl.ANY)],
        out_specs=[vmem, vmem],
        out_shape=[half, half],
        scratch_shapes=[
            pltpu.VMEM((rows, W), F32),
            pltpu.VMEM((3, 256, 256), F32),
            pltpu.SemaphoreType.DMA((rows // CHUNK,)),
        ],
        compiler_params=pltpu.CompilerParams(vmem_limit_bytes=52 * 1024 * 1024),
    )(core, spectra)


def tree(terms):
    while len(terms) > 1:
        terms = [terms[i] + terms[i + 1] if i + 1 < len(terms) else terms[i] for i in range(0, len(terms), 2)]
    return terms[0]


def lanes_of(group, lane):
    return jnp.broadcast_to(group[:, lane : lane + 1], (8, 128))


def row_of(group, i):
    return jnp.broadcast_to(group[i : i + 1, :], (8, 128))


def eliminate(a, one, out_ref):
    sub = lax.broadcasted_iota(jnp.int32, (8, 128), 0)
    square = [one * lanes_of(a[0], 64 + j) for j in range(8)]
    for b in range(8):
        lane = 64 + 8 * b
        near = {i: [lanes_of(a[i], lane + j) for j in range(8)] for i in range(b + 1, min(b + 3, 8))}
        following = []
        if b < 7:
            near[b + 1][0] = one * near[b + 1][0]
            following = [lanes_of(a[b + 1], lane + 8 + j) for j in range(8)]
        rows = a[b]
        scaled = []
        inverse = jnp.zeros((8, 128), F32)
        for k in range(8):
            s = {c: row_of(square[k], c) for c in range(k, 8)}
            inv = pl.reciprocal(s[k], approx=True)
            below = jnp.where(sub > k, square[k], 0.0)
            down = below * inv
            for c in range(k + 1, 8):
                square[c] = square[c] - ((below * s[c]) * inv if c == k + 1 else down * s[c])
            row = row_of(rows, k)
            rows = rows - down * row
            inverse = jnp.where(sub == k, inv, inverse)
            if b < 7:
                scaled.append(row * inv)
                for i, panel in near.items():
                    down = panel[k] * inv
                    for c in range(k + 1, 8):
                        panel[c] = panel[c] - down * s[c]
                    if i == b + 1:
                        for c in range(8):
                            following[c] = following[c] - down * row_of(panel[k], c)
        out_ref[8 * b : 8 * b + 8, :] = rows * (inverse * lax.rsqrt(inverse))
        if b == 7:
            break
        for i, panel in near.items():
            a[i] = a[i] - tree([panel[k] * scaled[k] for k in range(8)])
        panels = {i: [lanes_of(a[i], lane + j) for j in range(8)] for i in range(b + 3, 8)}
        if panels:
            q = rows * inverse
            for k in range(7, 0, -1):
                q = q - jnp.where(sub < k, square[k] * inverse, 0.0) * row_of(q, k)
            q = [row_of(q, c) for c in range(8)]
            for i, panel in panels.items():
                a[i] = a[i] - tree([panel[c] * q[c] for c in range(8)])
        square = following


def iterate_kernel(core_ref, mine_ref, other_ref, start_ref, spectra_ref, out_ref, gh, gl, basis, rp, sbuf, obuf, sem, osem):
    load = pltpu.make_async_copy(spectra_ref, sbuf, sem)
    load.start()
    core = core_ref[0]
    zero_is_mine = core == 0

    def put(i, j, value):
        at = (slice(128 * i, 128 * i + 128), slice(128 * j, 128 * j + 128))
        gh[at], gl[at] = split(value)

    for half in range(2):
        first, second = (mine_ref, other_ref) if half == 0 else (other_ref, mine_ref)
        for n, (i, j) in enumerate(BLOCKS[half]):
            at = slice(n * 128, n * 128 + 128)
            value = jnp.where(zero_is_mine, first[at, :], second[at, :]) * 2.0**-20
            flipped = value.T
            if i == j:
                value = value + flipped
            else:
                put(j, i, flipped)
            put(i, j, value)
    basis[...] = start_ref[...]
    lanes = lax.broadcasted_iota(jnp.int32, (K, 128), 1)
    eye = (lanes == lax.broadcasted_iota(jnp.int32, (K, 128), 0)).astype(F32)

    one = jnp.where(core >= 0, 1.0, 0.0)

    def step(_, carry):
        bh, bl = split(basis[...])
        both = mul(jnp.concatenate([bh, bl], axis=0), gh[...], NN)
        image = both[:K] + both[K:] + mul(bh, gl[...], NN)
        ih, il = split(image)
        first = mul(jnp.concatenate([ih, il], axis=0), jnp.concatenate([il, ih], axis=0), NT)
        cross = first[:K] + first[K:] + mul(ih, jnp.concatenate([ih, il], axis=0), NT)
        a = jnp.where(lanes < K, eye, cross)
        eliminate([a[8 * i : 8 * i + 8, :] for i in range(8)], one, rp)
        xh, xl = split(rp[:, :K])
        both = mul(jnp.concatenate([xh, xl], axis=0), ih, NN)
        basis[...] = both[:K] + both[K:] + mul(xh, il, NN)
        return carry

    lax.fori_loop(0, ITERS, step, 0)
    bh, bl = split(basis[...])
    load.wait()
    both = jnp.concatenate([bh, bl], axis=0)
    rows = 512
    stores = []
    for i in range(sbuf.shape[0] // rows):
        at = slice(i * rows, i * rows + rows)
        sh, sl = split(sbuf[at, :])
        wide = mul(both, sh, NT)
        obuf[:, at] = wide[:K] + wide[K:] + mul(bh, sl, NT)
        stores.append(pltpu.make_async_copy(obuf.at[:, at], out_ref.at[:, at], osem.at[i]))
        stores[-1].start()
    for store in stores:
        store.wait()


def finish(core, mine, other, start, spectra):
    rows = spectra.shape[0]
    vmem = pl.BlockSpec(memory_space=pltpu.VMEM)
    hbm = pl.BlockSpec(memory_space=pl.ANY)
    return pl.pallas_call(
        iterate_kernel,
        in_specs=[pl.BlockSpec(memory_space=pltpu.SMEM), vmem, vmem, vmem, hbm],
        out_specs=hbm,
        out_shape=jax.ShapeDtypeStruct((K, rows), F32),
        scratch_shapes=[
            pltpu.VMEM((W, W), BF16),
            pltpu.VMEM((W, W), BF16),
            pltpu.VMEM((K, W), F32),
            pltpu.VMEM((K, 128), F32),
            pltpu.VMEM((rows, W), F32),
            pltpu.VMEM((K, rows), F32),
            pltpu.SemaphoreType.DMA,
            pltpu.SemaphoreType.DMA((rows // 512,)),
        ],
        compiler_params=pltpu.CompilerParams(vmem_limit_bytes=52 * 1024 * 1024),
    )(core, mine, other, start, spectra)


def swap(value):
    return lax.ppermute(value, "core", [(0, 1), (1, 0)])


def spread(piece, axis, copies):
    return lax.all_to_all(jnp.broadcast_to(piece[None], (copies, *piece.shape)), axis, 0, 0)


def body(raster, z, spectra, start):
    core = lax.axis_index("core").astype(jnp.int32).reshape(1)
    keep, send = gram_halves(core, spectra)
    part = keep + swap(send)
    part = lax.all_to_all(part.reshape(raster, 1, HALF * 128 // raster), "raster", 0, 0)
    piece = jnp.sum(part, axis=0)
    piece = jnp.sum(spread(piece, "z", z), axis=0)
    mine = spread(piece, "raster", raster).reshape(HALF, 128)
    return finish(core, mine, swap(mine), start.T, spectra).T


def solution(mesh):
    raster, slit = mesh.devices.shape
    inner = Mesh(mesh.devices.reshape(raster, slit // 2, 2), ("raster", "z", "core"))
    rows = P(("raster", "z", "core"), None)
    return jax.shard_map(
        functools.partial(body, raster, slit // 2),
        mesh=inner,
        in_specs=(rows, P()),
        out_specs=rows,
        check_vma=False,
    )
```

```python
import functools

import jax
import jax.numpy as jnp
from jax import lax
from jax.experimental import pallas as pl
from jax.experimental.pallas import tpu as pltpu
from jax.sharding import Mesh, PartitionSpec as P

W = 512
K = 64
ITERS = 6
CHUNK = 512
HALF = 5 * 128
BLOCKS = (((0, 0), (0, 1), (0, 2), (0, 3), (3, 3)), ((1, 1), (1, 2), (1, 3), (2, 2), (2, 3)))
F32 = jnp.float32
BF16 = jnp.bfloat16
NN = (((1,), (0,)), ((), ()))
NT = (((1,), (1,)), ((), ()))
TN = (((0,), (0,)), ((), ()))


def mul(a, b, dims):
    return lax.dot_general(a, b, dims, preferred_element_type=F32)


def split(value):
    high = value.astype(BF16)
    return high, (value - high.astype(F32)).astype(BF16)


def gram_kernel(core_ref, spectra_ref, keep_ref, send_ref, buf, acc, sems):
    parts = buf.shape[0] // CHUNK
    loads = []
    for i in range(parts):
        at = slice(i * CHUNK, i * CHUNK + CHUNK)
        loads.append(pltpu.make_async_copy(spectra_ref.at[at], buf.at[at], sems.at[i]))
        loads[-1].start()
    for i in range(parts):
        loads[i].wait()
        high, low = split(buf[i * CHUNK : i * CHUNK + CHUNK, :])
        h0, h1 = high[:, :256], high[:, 256:]
        l0, l1 = low[:, :256], low[:, 256:]
        sums = (
            0.5 * mul(h0, h0, TN) + mul(h0, l0, TN),
            mul(h0, h1, TN) + mul(h0, l1, TN) + mul(l0, h1, TN),
            0.5 * mul(h1, h1, TN) + mul(h1, l1, TN),
        )
        for block in range(3):
            acc[block] = acc[block] + sums[block] if i else sums[block]

    def block(i, j):
        rows, columns = i % 2 * 128, j % 2 * 128
        return acc[i // 2 + j // 2, rows : rows + 128, columns : columns + 128]

    def put(ref, half):
        for n, (i, j) in enumerate(BLOCKS[half]):
            value = block(i, j)
            if i != j and i // 2 == j // 2:
                value = value + block(j, i).T
            ref[n * 128 : n * 128 + 128, :] = value

    for core in range(2):

        @pl.when(core_ref[0] == core)
        def _():
            put(keep_ref, core)
            put(send_ref, 1 - core)


def gram_halves(core, spectra):
    rows = spectra.shape[0]
    half = jax.ShapeDtypeStruct((HALF, 128), F32)
    vmem = pl.BlockSpec(memory_space=pltpu.VMEM)
    return pl.pallas_call(
        gram_kernel,
        in_specs=[pl.BlockSpec(memory_space=pltpu.SMEM), pl.BlockSpec(memory_space=pl.ANY)],
        out_specs=[vmem, vmem],
        out_shape=[half, half],
        scratch_shapes=[
            pltpu.VMEM((rows, W), F32),
            pltpu.VMEM((3, 256, 256), F32),
            pltpu.SemaphoreType.DMA((rows // CHUNK,)),
        ],
        compiler_params=pltpu.CompilerParams(vmem_limit_bytes=52 * 1024 * 1024),
    )(core, spectra)


def tree(terms):
    while len(terms) > 1:
        terms = [terms[i] + terms[i + 1] if i + 1 < len(terms) else terms[i] for i in range(0, len(terms), 2)]
    return terms[0]


def lanes_of(group, lane):
    return jnp.broadcast_to(group[:, lane : lane + 1], (8, 128))


def row_of(group, i):
    return jnp.broadcast_to(group[i : i + 1, :], (8, 128))


def eliminate(a, one, out_ref):
    sub = lax.broadcasted_iota(jnp.int32, (8, 128), 0)
    square = [one * lanes_of(a[0], 64 + j) for j in range(8)]
    for b in range(8):
        lane = 64 + 8 * b
        panels = {i: [lanes_of(a[i], lane + j) for j in range(8)] for i in range(b + 1, 8)}
        following = []
        if b < 7:
            panels[b + 1][0] = one * panels[b + 1][0]
            following = [lanes_of(a[b + 1], lane + 8 + j) for j in range(8)]
        rows = a[b]
        inverse = jnp.zeros((8, 128), F32)
        for p in range(0, 8, 2):
            q = p + 1
            first = {c: row_of(square[p], c) for c in range(p, 8)}
            second = {c: row_of(square[q], c) for c in range(q, 8)}
            cofactor = pl.reciprocal(first[p] * second[q] - first[q] * first[q], approx=True)
            invs = (pl.reciprocal(first[p], approx=True), first[p] * cofactor)
            for c in range(q + 1, min(q + 3, 8)):
                left = second[q] * first[c] - first[q] * second[c]
                right = first[p] * second[c] - first[q] * first[c]
                square[c] = square[c] - (square[p] * left + square[q] * right) * cofactor
            downs = [jnp.where(sub > p, square[p], 0.0) * invs[0]]
            square[q] = square[q] - downs[0] * first[q]
            downs.append(jnp.where(sub > q, square[q], 0.0) * invs[1])
            second = {c: row_of(square[q], c) for c in range(q + 1, 8)}
            for c in range(q + 3, 8):
                square[c] = (square[c] - downs[0] * first[c]) - downs[1] * second[c]
            for k, s, inv, down in zip((p, q), (first, second), invs, downs):
                row = row_of(rows, k)
                rows = rows - down * row
                inverse = jnp.where(sub == k, inv, inverse)
                for i, panel in panels.items():
                    down = panel[k] * inv
                    for c in range(k + 1, 8):
                        panel[c] = panel[c] - down * s[c]
                    if i == b + 1:
                        for c in range(8):
                            following[c] = following[c] - down * row_of(panel[k], c)
                    a[i] = a[i] - down * row
        out_ref[8 * b : 8 * b + 8, :] = rows * (inverse * lax.rsqrt(inverse))
        square = following


def iterate_kernel(core_ref, mine_ref, other_ref, start_ref, spectra_ref, out_ref, gh, gl, basis, rp, sbuf, obuf, sem, osem):
    load = pltpu.make_async_copy(spectra_ref, sbuf, sem)
    load.start()
    core = core_ref[0]
    zero_is_mine = core == 0

    def put(i, j, value):
        at = (slice(128 * i, 128 * i + 128), slice(128 * j, 128 * j + 128))
        gh[at], gl[at] = split(value)

    for half in range(2):
        first, second = (mine_ref, other_ref) if half == 0 else (other_ref, mine_ref)
        for n, (i, j) in enumerate(BLOCKS[half]):
            at = slice(n * 128, n * 128 + 128)
            value = jnp.where(zero_is_mine, first[at, :], second[at, :]) * 2.0**-20
            flipped = value.T
            if i == j:
                value = value + flipped
            else:
                put(j, i, flipped)
            put(i, j, value)
    def times_gram(high, low):
        both = mul(jnp.concatenate([high, low], axis=0), gh[...], NN)
        return both[:K] + both[K:] + mul(high, gl[...], NN)

    basis[...] = times_gram(*split(start_ref[...]))
    lanes = lax.broadcasted_iota(jnp.int32, (K, 128), 1)
    eye = (lanes == lax.broadcasted_iota(jnp.int32, (K, 128), 0)).astype(F32)

    one = jnp.where(core >= 0, 1.0, 0.0)

    def step(count, carry):
        image = basis[...]
        ih, il = split(image)
        first = mul(jnp.concatenate([ih, il], axis=0), jnp.concatenate([il, ih], axis=0), NT)
        cross = first[:K] + first[K:] + mul(ih, jnp.concatenate([ih, il], axis=0), NT)
        a = jnp.where(lanes < K, eye, cross)
        wh, wl = split(jnp.where(count == ITERS - 1, image, times_gram(ih, il)))
        eliminate([a[8 * i : 8 * i + 8, :] for i in range(8)], one, rp)
        xh, xl = split(rp[:, :K])
        both = mul(jnp.concatenate([xh, xl], axis=0), wh, NN)
        basis[...] = both[:K] + both[K:] + mul(xh, wl, NN)
        return carry

    lax.fori_loop(0, ITERS, step, 0)
    bh, bl = split(basis[...])
    load.wait()
    both = jnp.concatenate([bh, bl], axis=0)
    rows = 512
    stores = []
    for i in range(sbuf.shape[0] // rows):
        at = slice(i * rows, i * rows + rows)
        sh, sl = split(sbuf[at, :])
        wide = mul(both, sh, NT)
        obuf[:, at] = wide[:K] + wide[K:] + mul(bh, sl, NT)
        stores.append(pltpu.make_async_copy(obuf.at[:, at], out_ref.at[:, at], osem.at[i]))
        stores[-1].start()
    for store in stores:
        store.wait()


def finish(core, mine, other, start, spectra):
    rows = spectra.shape[0]
    vmem = pl.BlockSpec(memory_space=pltpu.VMEM)
    hbm = pl.BlockSpec(memory_space=pl.ANY)
    return pl.pallas_call(
        iterate_kernel,
        in_specs=[pl.BlockSpec(memory_space=pltpu.SMEM), vmem, vmem, vmem, hbm],
        out_specs=hbm,
        out_shape=jax.ShapeDtypeStruct((K, rows), F32),
        scratch_shapes=[
            pltpu.VMEM((W, W), BF16),
            pltpu.VMEM((W, W), BF16),
            pltpu.VMEM((K, W), F32),
            pltpu.VMEM((K, 128), F32),
            pltpu.VMEM((rows, W), F32),
            pltpu.VMEM((K, rows), F32),
            pltpu.SemaphoreType.DMA,
            pltpu.SemaphoreType.DMA((rows // 512,)),
        ],
        compiler_params=pltpu.CompilerParams(vmem_limit_bytes=52 * 1024 * 1024),
    )(core, mine, other, start, spectra)


def swap(value):
    return lax.ppermute(value, "core", [(0, 1), (1, 0)])


def spread(piece, axis, copies):
    return lax.all_to_all(jnp.broadcast_to(piece[None], (copies, *piece.shape)), axis, 0, 0)


def body(raster, z, spectra, start):
    core = lax.axis_index("core").astype(jnp.int32).reshape(1)
    keep, send = gram_halves(core, spectra)
    part = keep + swap(send)
    part = lax.all_to_all(part.reshape(raster, 1, HALF * 128 // raster), "raster", 0, 0)
    piece = jnp.sum(part, axis=0)
    piece = jnp.sum(spread(piece, "z", z), axis=0)
    mine = spread(piece, "raster", raster).reshape(HALF, 128)
    return finish(core, mine, swap(mine), start.T, spectra).T


def solution(mesh):
    raster, slit = mesh.devices.shape
    inner = Mesh(mesh.devices.reshape(raster, slit // 2, 2), ("raster", "z", "core"))
    rows = P(("raster", "z", "core"), None)
    return jax.shard_map(
        functools.partial(body, raster, slit // 2),
        mesh=inner,
        in_specs=(rows, P()),
        out_specs=rows,
        check_vma=False,
    )
```

```python
import functools

import jax
import jax.numpy as jnp
from jax import lax
from jax.experimental import pallas as pl
from jax.experimental.pallas import tpu as pltpu
from jax.sharding import Mesh, PartitionSpec as P

W = 512
K = 64
ITERS = 6
CHUNK = 512
HALF = 3 * 128 + 3 * 64
OFF = (((0, 1), (0, 2), (0, 3)), ((1, 2), (1, 3), (2, 3)))
F32 = jnp.float32
BF16 = jnp.bfloat16
NN = (((1,), (0,)), ((), ()))
NT = (((1,), (1,)), ((), ()))
TN = (((0,), (0,)), ((), ()))


def mul(a, b, dims):
    return lax.dot_general(a, b, dims, preferred_element_type=F32)


def split(value):
    high = value.astype(BF16)
    return high, (value - high.astype(F32)).astype(BF16)


def gram_kernel(core_ref, spectra_ref, keep_ref, send_ref, buf, acc, sems):
    parts = buf.shape[0] // CHUNK
    loads = []
    for i in range(parts):
        at = slice(i * CHUNK, i * CHUNK + CHUNK)
        loads.append(pltpu.make_async_copy(spectra_ref.at[at], buf.at[at], sems.at[i]))
        loads[-1].start()
    for i in range(parts):
        loads[i].wait()
        high, low = split(buf[i * CHUNK : i * CHUNK + CHUNK, :])
        h0, h1 = high[:, :256], high[:, 256:]
        l0, l1 = low[:, :256], low[:, 256:]
        sums = (
            0.5 * mul(h0, h0, TN) + mul(h0, l0, TN),
            mul(h0, h1, TN) + mul(h0, l1, TN) + mul(l0, h1, TN),
            0.5 * mul(h1, h1, TN) + mul(h1, l1, TN),
        )
        for block in range(3):
            acc[block] = acc[block] + sums[block] if i else sums[block]

    def block(i, j):
        rows, columns = i % 2 * 128, j % 2 * 128
        return acc[i // 2 + j // 2, rows : rows + 128, columns : columns + 128]

    def put(ref, half):
        for n, (i, j) in enumerate(OFF[half]):
            value = block(i, j)
            if i // 2 == j // 2:
                value = value + block(j, i).T
            ref[n * 128 : n * 128 + 128, :] = value
        right = lax.broadcasted_iota(jnp.int32, (64, 128), 1) >= 64
        corners = []
        for n, i in enumerate((2 * half, 2 * half + 1)):
            value = block(i, i)
            at = 384 + n * 64
            ref[at : at + 64, :] = value[:64] + jnp.where(right, value.T[:64], 0.0)
            corners.append(value[64:])
        ref[512:576, :] = jnp.where(right, corners[1], pltpu.roll(corners[0], 64, 1))

    for core in range(2):

        @pl.when(core_ref[0] == core)
        def _():
            put(keep_ref, core)
            put(send_ref, 1 - core)


def gram_halves(core, spectra):
    rows = spectra.shape[0]
    half = jax.ShapeDtypeStruct((HALF, 128), F32)
    vmem = pl.BlockSpec(memory_space=pltpu.VMEM)
    return pl.pallas_call(
        gram_kernel,
        in_specs=[pl.BlockSpec(memory_space=pltpu.SMEM), pl.BlockSpec(memory_space=pl.ANY)],
        out_specs=[vmem, vmem],
        out_shape=[half, half],
        scratch_shapes=[
            pltpu.VMEM((rows, W), F32),
            pltpu.VMEM((3, 256, 256), F32),
            pltpu.SemaphoreType.DMA((rows // CHUNK,)),
        ],
        compiler_params=pltpu.CompilerParams(vmem_limit_bytes=52 * 1024 * 1024),
    )(core, spectra)


def tree(terms):
    while len(terms) > 1:
        terms = [terms[i] + terms[i + 1] if i + 1 < len(terms) else terms[i] for i in range(0, len(terms), 2)]
    return terms[0]


def lanes_of(group, lane):
    return jnp.broadcast_to(group[:, lane : lane + 1], (8, 128))


def row_of(group, i):
    return jnp.broadcast_to(group[i : i + 1, :], (8, 128))


def eliminate(a, one, out_ref):
    sub = lax.broadcasted_iota(jnp.int32, (8, 128), 0)
    square = [one * lanes_of(a[0], 64 + j) for j in range(8)]
    for b in range(8):
        lane = 64 + 8 * b
        panels = {i: [lanes_of(a[i], lane + j) for j in range(8)] for i in range(b + 1, 8)}
        following = []
        if b < 7:
            panels[b + 1][0] = one * panels[b + 1][0]
            following = [lanes_of(a[b + 1], lane + 8 + j) for j in range(8)]
        rows = a[b]
        inverse = jnp.zeros((8, 128), F32)
        for p in range(0, 8, 2):
            q = p + 1
            first = {c: row_of(square[p], c) for c in range(p, 8)}
            second = {c: row_of(square[q], c) for c in range(q, 8)}
            cofactor = pl.reciprocal(first[p] * second[q] - first[q] * first[q], approx=True)
            invs = (pl.reciprocal(first[p], approx=True), first[p] * cofactor)
            for c in range(q + 1, min(q + 3, 8)):
                left = second[q] * first[c] - first[q] * second[c]
                right = first[p] * second[c] - first[q] * first[c]
                square[c] = square[c] - (square[p] * left + square[q] * right) * cofactor
            downs = [jnp.where(sub > p, square[p], 0.0) * invs[0]]
            square[q] = square[q] - downs[0] * first[q]
            downs.append(jnp.where(sub > q, square[q], 0.0) * invs[1])
            second = {c: row_of(square[q], c) for c in range(q + 1, 8)}
            for c in range(q + 3, 8):
                square[c] = (square[c] - downs[0] * first[c]) - downs[1] * second[c]
            for k, s, inv, down in zip((p, q), (first, second), invs, downs):
                row = row_of(rows, k)
                rows = rows - down * row
                inverse = jnp.where(sub == k, inv, inverse)
                for i, panel in panels.items():
                    down = panel[k] * inv
                    for c in range(k + 1, 8):
                        panel[c] = panel[c] - down * s[c]
                    if i == b + 1:
                        for c in range(8):
                            following[c] = following[c] - down * row_of(panel[k], c)
                    a[i] = a[i] - down * row
        out_ref[8 * b : 8 * b + 8, :] = rows * (inverse * lax.rsqrt(inverse))
        square = following


def iterate_kernel(core_ref, mine_ref, other_ref, start_ref, spectra_ref, out_ref, gh, gl, basis, rp, sbuf, obuf, sem, osem):
    load = pltpu.make_async_copy(spectra_ref, sbuf, sem)
    load.start()
    core = core_ref[0]
    zero_is_mine = core == 0

    def put(i, j, value):
        at = (slice(128 * i, 128 * i + 128), slice(128 * j, 128 * j + 128))
        gh[at], gl[at] = split(value)

    right = lax.broadcasted_iota(jnp.int32, (64, 128), 1) >= 64
    for half in range(2):
        first, second = (mine_ref, other_ref) if half == 0 else (other_ref, mine_ref)

        def rows_at(start, count):
            at = slice(start, start + count)
            return jnp.where(zero_is_mine, first[at, :], second[at, :]) * 2.0**-20

        for n, (i, j) in enumerate(OFF[half]):
            value = rows_at(n * 128, 128)
            put(i, j, value)
            put(j, i, value.T)
        corners = rows_at(512, 64)
        for n, i in enumerate((2 * half, 2 * half + 1)):
            corner = jnp.where(right, corners if n else pltpu.roll(corners, 64, 1), 0.0)
            value = jnp.concatenate([rows_at(384 + n * 64, 64), corner], axis=0)
            put(i, i, value + value.T)

    def times_gram(high, low):
        both = mul(jnp.concatenate([high, low], axis=0), gh[...], NN)
        return both[:K] + both[K:] + mul(high, gl[...], NN)

    basis[...] = times_gram(*split(start_ref[...]))
    lanes = lax.broadcasted_iota(jnp.int32, (K, 128), 1)
    eye = (lanes == lax.broadcasted_iota(jnp.int32, (K, 128), 0)).astype(F32)

    one = jnp.where(core >= 0, 1.0, 0.0)

    def step(count, carry):
        image = basis[...]
        ih, il = split(image)
        first = mul(jnp.concatenate([ih, il], axis=0), jnp.concatenate([il, ih], axis=0), NT)
        cross = first[:K] + first[K:] + mul(ih, jnp.concatenate([ih, il], axis=0), NT)
        a = jnp.where(lanes < K, eye, cross)
        wh, wl = split(jnp.where(count == ITERS - 1, image, times_gram(ih, il)))
        eliminate([a[8 * i : 8 * i + 8, :] for i in range(8)], one, rp)
        xh, xl = split(rp[:, :K])
        both = mul(jnp.concatenate([xh, xl], axis=0), wh, NN)
        basis[...] = both[:K] + both[K:] + mul(xh, wl, NN)
        return carry

    lax.fori_loop(0, ITERS, step, 0)
    bh, bl = split(basis[...])
    load.wait()
    both = jnp.concatenate([bh, bl], axis=0)
    rows = 512
    stores = []
    for i in range(sbuf.shape[0] // rows):
        at = slice(i * rows, i * rows + rows)
        sh, sl = split(sbuf[at, :])
        wide = mul(both, sh, NT)
        obuf[:, at] = wide[:K] + wide[K:] + mul(bh, sl, NT)
        stores.append(pltpu.make_async_copy(obuf.at[:, at], out_ref.at[:, at], osem.at[i]))
        stores[-1].start()
    for store in stores:
        store.wait()


def finish(core, mine, other, start, spectra):
    rows = spectra.shape[0]
    vmem = pl.BlockSpec(memory_space=pltpu.VMEM)
    hbm = pl.BlockSpec(memory_space=pl.ANY)
    return pl.pallas_call(
        iterate_kernel,
        in_specs=[pl.BlockSpec(memory_space=pltpu.SMEM), vmem, vmem, vmem, hbm],
        out_specs=hbm,
        out_shape=jax.ShapeDtypeStruct((K, rows), F32),
        scratch_shapes=[
            pltpu.VMEM((W, W), BF16),
            pltpu.VMEM((W, W), BF16),
            pltpu.VMEM((K, W), F32),
            pltpu.VMEM((K, 128), F32),
            pltpu.VMEM((rows, W), F32),
            pltpu.VMEM((K, rows), F32),
            pltpu.SemaphoreType.DMA,
            pltpu.SemaphoreType.DMA((rows // 512,)),
        ],
        compiler_params=pltpu.CompilerParams(vmem_limit_bytes=52 * 1024 * 1024),
    )(core, mine, other, start, spectra)


def swap(value):
    return lax.ppermute(value, "core", [(0, 1), (1, 0)])


def spread(piece, axis, copies):
    return lax.all_to_all(jnp.broadcast_to(piece[None], (copies, *piece.shape)), axis, 0, 0)


def body(raster, z, spectra, start):
    core = lax.axis_index("core").astype(jnp.int32).reshape(1)
    keep, send = gram_halves(core, spectra)
    part = keep + swap(send)
    part = lax.all_to_all(part.reshape(raster, 1, HALF * 128 // raster), "raster", 0, 0)
    piece = jnp.sum(part, axis=0)
    piece = jnp.sum(spread(piece, "z", z), axis=0)
    mine = spread(piece, "raster", raster).reshape(HALF, 128)
    return finish(core, mine, swap(mine), start.T, spectra).T


def solution(mesh):
    raster, slit = mesh.devices.shape
    inner = Mesh(mesh.devices.reshape(raster, slit // 2, 2), ("raster", "z", "core"))
    rows = P(("raster", "z", "core"), None)
    return jax.shard_map(
        functools.partial(body, raster, slit // 2),
        mesh=inner,
        in_specs=(rows, P()),
        out_specs=rows,
        check_vma=False,
    )
```

```python
import functools

import jax
import jax.numpy as jnp
from jax import lax
from jax.experimental import pallas as pl
from jax.experimental.pallas import tpu as pltpu
from jax.sharding import Mesh, PartitionSpec as P

W = 512
K = 64
ITERS = 6
NEAR = (5, 8, 8, 8, 8, 8, 8, 8)
CHUNKS = (256, 768, 1024)
HALF = 3 * 128 + 3 * 64
OFF = (((0, 1), (0, 2), (0, 3)), ((1, 2), (1, 3), (2, 3)))
F32 = jnp.float32
BF16 = jnp.bfloat16
NN = (((1,), (0,)), ((), ()))
NT = (((1,), (1,)), ((), ()))
TN = (((0,), (0,)), ((), ()))


def mul(a, b, dims):
    return lax.dot_general(a, b, dims, preferred_element_type=F32)


def split(value):
    high = value.astype(BF16)
    return high, (value - high.astype(F32)).astype(BF16)


def gram_kernel(core_ref, spectra_ref, keep_ref, send_ref, buf, acc, sems):
    loads = []
    start = 0
    for n, rows in enumerate(CHUNKS):
        at = slice(start, start + rows)
        start += rows
        loads.append((at, pltpu.make_async_copy(spectra_ref.at[at], buf.at[at], sems.at[n])))
        loads[-1][1].start()
    for n, (at, load) in enumerate(loads):
        load.wait()
        high, low = split(buf[at, :])
        h0, h1 = high[:, :256], high[:, 256:]
        l0, l1 = low[:, :256], low[:, 256:]
        sums = (
            0.5 * mul(h0, h0, TN) + mul(h0, l0, TN),
            mul(h0, h1, TN) + mul(h0, l1, TN) + mul(l0, h1, TN),
            0.5 * mul(h1, h1, TN) + mul(h1, l1, TN),
        )
        for block in range(3):
            acc[block] = acc[block] + sums[block] if n else sums[block]

    def block(i, j):
        rows, columns = i % 2 * 128, j % 2 * 128
        return acc[i // 2 + j // 2, rows : rows + 128, columns : columns + 128]

    def put(ref, half):
        for n, (i, j) in enumerate(OFF[half]):
            value = block(i, j)
            if i // 2 == j // 2:
                value = value + block(j, i).T
            ref[n * 128 : n * 128 + 128, :] = value
        right = lax.broadcasted_iota(jnp.int32, (64, 128), 1) >= 64
        corners = []
        for n, i in enumerate((2 * half, 2 * half + 1)):
            value = block(i, i)
            at = 384 + n * 64
            ref[at : at + 64, :] = value[:64] + jnp.where(right, value.T[:64], 0.0)
            corners.append(value[64:])
        ref[512:576, :] = jnp.where(right, corners[1], pltpu.roll(corners[0], 64, 1))

    for core in range(2):

        @pl.when(core_ref[0] == core)
        def _():
            put(keep_ref, core)
            put(send_ref, 1 - core)


def gram_halves(core, spectra):
    rows = spectra.shape[0]
    half = jax.ShapeDtypeStruct((HALF, 128), F32)
    vmem = pl.BlockSpec(memory_space=pltpu.VMEM)
    return pl.pallas_call(
        gram_kernel,
        in_specs=[pl.BlockSpec(memory_space=pltpu.SMEM), pl.BlockSpec(memory_space=pl.ANY)],
        out_specs=[vmem, vmem],
        out_shape=[half, half],
        scratch_shapes=[
            pltpu.VMEM((rows, W), F32),
            pltpu.VMEM((3, 256, 256), F32),
            pltpu.SemaphoreType.DMA((len(CHUNKS),)),
        ],
        compiler_params=pltpu.CompilerParams(vmem_limit_bytes=52 * 1024 * 1024),
    )(core, spectra)


def tree(terms):
    while len(terms) > 1:
        terms = [terms[i] + terms[i + 1] if i + 1 < len(terms) else terms[i] for i in range(0, len(terms), 2)]
    return terms[0]


def lanes_of(group, lane):
    return jnp.broadcast_to(group[:, lane : lane + 1], (8, 128))


def row_of(group, i):
    return jnp.broadcast_to(group[i : i + 1, :], (8, 128))


def eliminate(a, one, out_ref):
    sub = lax.broadcasted_iota(jnp.int32, (8, 128), 0)
    square = [one * lanes_of(a[0], 64 + j) for j in range(8)]
    for b in range(8):
        lane = 64 + 8 * b
        panels = {i: [lanes_of(a[i], lane + j) for j in range(8)] for i in range(b + 1, min(b + NEAR[b], 8))}
        following = []
        if b < 7:
            panels[b + 1][0] = one * panels[b + 1][0]
            following = [lanes_of(a[b + 1], lane + 8 + j) for j in range(8)]
        rows = a[b]
        inverse = jnp.zeros((8, 128), F32)
        upper = [jnp.zeros((8, 128), F32)] * 8
        for p in range(0, 8, 2):
            q = p + 1
            first = {c: row_of(square[p], c) for c in range(p, 8)}
            second = {c: row_of(square[q], c) for c in range(q, 8)}
            cofactor = pl.reciprocal(first[p] * second[q] - first[q] * first[q], approx=True)
            invs = (pl.reciprocal(first[p], approx=True), first[p] * cofactor)
            for c in range(q + 1, min(q + 3, 8)):
                left = second[q] * first[c] - first[q] * second[c]
                right = first[p] * second[c] - first[q] * first[c]
                square[c] = square[c] - (square[p] * left + square[q] * right) * cofactor
            downs = [jnp.where(sub > p, square[p], 0.0) * invs[0]]
            square[q] = square[q] - downs[0] * first[q]
            downs.append(jnp.where(sub > q, square[q], 0.0) * invs[1])
            second = {c: row_of(square[q], c) for c in range(q + 1, 8)}
            for c in range(q + 3, 8):
                square[c] = (square[c] - downs[0] * first[c]) - downs[1] * second[c]
            for k, s, inv, down in zip((p, q), (first, second), invs, downs):
                row = row_of(rows, k)
                rows = rows - down * row
                inverse = jnp.where(sub == k, inv, inverse)
                for c in range(k + 1, 8) if b + NEAR[b] < 8 else ():
                    upper[c] = jnp.where(sub == k, s[c], upper[c])
                for i, panel in panels.items():
                    down = panel[k] * inv
                    for c in range(k + 1, 8):
                        panel[c] = panel[c] - down * s[c]
                    if i == b + 1:
                        for c in range(8):
                            following[c] = following[c] - down * row_of(panel[k], c)
                    a[i] = a[i] - down * row
        out_ref[8 * b : 8 * b + 8, :] = rows * (inverse * lax.rsqrt(inverse))
        if b + NEAR[b] < 8:
            q = rows * inverse
            for c in range(7, 0, -1):
                q = q - upper[c] * inverse * row_of(q, c)
            q = [row_of(q, c) for c in range(8)]
            for i in range(b + NEAR[b], 8):
                a[i] = a[i] - tree([lanes_of(a[i], lane + c) * q[c] for c in range(8)])
        square = following


def iterate_kernel(core_ref, mine_ref, other_ref, start_ref, spectra_ref, out_ref, gh, gl, basis, rp, sbuf, obuf, sem, osem):
    load = pltpu.make_async_copy(spectra_ref, sbuf, sem)
    load.start()
    core = core_ref[0]
    zero_is_mine = core == 0

    def put(i, j, value):
        at = (slice(128 * i, 128 * i + 128), slice(128 * j, 128 * j + 128))
        gh[at], gl[at] = split(value)

    right = lax.broadcasted_iota(jnp.int32, (64, 128), 1) >= 64
    for half in range(2):
        first, second = (mine_ref, other_ref) if half == 0 else (other_ref, mine_ref)

        def rows_at(start, count):
            at = slice(start, start + count)
            return jnp.where(zero_is_mine, first[at, :], second[at, :]) * 2.0**-20

        for n, (i, j) in enumerate(OFF[half]):
            value = rows_at(n * 128, 128)
            put(i, j, value)
            put(j, i, value.T)
        corners = rows_at(512, 64)
        for n, i in enumerate((2 * half, 2 * half + 1)):
            corner = jnp.where(right, corners if n else pltpu.roll(corners, 64, 1), 0.0)
            value = jnp.concatenate([rows_at(384 + n * 64, 64), corner], axis=0)
            put(i, i, value + value.T)

    def times_gram(high, low):
        both = mul(jnp.concatenate([high, low], axis=0), gh[...], NN)
        return both[:K] + both[K:] + mul(high, gl[...], NN)

    basis[...] = times_gram(*split(start_ref[...]))
    lanes = lax.broadcasted_iota(jnp.int32, (K, 128), 1)
    eye = (lanes == lax.broadcasted_iota(jnp.int32, (K, 128), 0)).astype(F32)

    one = jnp.where(core >= 0, 1.0, 0.0)

    def step(count, carry):
        image = basis[...]
        ih, il = split(image)
        first = mul(jnp.concatenate([ih, il], axis=0), jnp.concatenate([il, ih], axis=0), NT)
        cross = first[:K] + first[K:] + mul(ih, jnp.concatenate([ih, il], axis=0), NT)
        a = jnp.where(lanes < K, eye, cross)
        wh, wl = split(jnp.where(count == ITERS - 1, image, times_gram(ih, il)))
        eliminate([a[8 * i : 8 * i + 8, :] for i in range(8)], one, rp)
        xh, xl = split(rp[:, :K])
        both = mul(jnp.concatenate([xh, xl], axis=0), wh, NN)
        basis[...] = both[:K] + both[K:] + mul(xh, wl, NN)
        return carry

    lax.fori_loop(0, ITERS, step, 0)
    bh, bl = split(basis[...])
    load.wait()
    both = jnp.concatenate([bh, bl], axis=0)
    rows = 512
    stores = []
    for i in range(sbuf.shape[0] // rows):
        at = slice(i * rows, i * rows + rows)
        sh, sl = split(sbuf[at, :])
        wide = mul(both, sh, NT)
        obuf[:, at] = wide[:K] + wide[K:] + mul(bh, sl, NT)
        stores.append(pltpu.make_async_copy(obuf.at[:, at], out_ref.at[:, at], osem.at[i]))
        stores[-1].start()
    for store in stores:
        store.wait()


def finish(core, mine, other, start, spectra):
    rows = spectra.shape[0]
    vmem = pl.BlockSpec(memory_space=pltpu.VMEM)
    hbm = pl.BlockSpec(memory_space=pl.ANY)
    return pl.pallas_call(
        iterate_kernel,
        in_specs=[pl.BlockSpec(memory_space=pltpu.SMEM), vmem, vmem, vmem, hbm],
        out_specs=hbm,
        out_shape=jax.ShapeDtypeStruct((K, rows), F32),
        scratch_shapes=[
            pltpu.VMEM((W, W), BF16),
            pltpu.VMEM((W, W), BF16),
            pltpu.VMEM((K, W), F32),
            pltpu.VMEM((K, 128), F32),
            pltpu.VMEM((rows, W), F32),
            pltpu.VMEM((K, rows), F32),
            pltpu.SemaphoreType.DMA,
            pltpu.SemaphoreType.DMA((rows // 512,)),
        ],
        compiler_params=pltpu.CompilerParams(vmem_limit_bytes=52 * 1024 * 1024),
    )(core, mine, other, start, spectra)


def swap(value):
    return lax.ppermute(value, "core", [(0, 1), (1, 0)])


def spread(piece, axis, copies):
    return lax.all_to_all(jnp.broadcast_to(piece[None], (copies, *piece.shape)), axis, 0, 0)


def body(raster, z, spectra, start):
    core = lax.axis_index("core").astype(jnp.int32).reshape(1)
    keep, send = gram_halves(core, spectra)
    part = keep + swap(send)
    part = lax.all_to_all(part.reshape(raster, 1, HALF * 128 // raster), "raster", 0, 0)
    piece = jnp.sum(part, axis=0)
    piece = jnp.sum(spread(piece, "z", z), axis=0)
    mine = spread(piece, "raster", raster).reshape(HALF, 128)
    return finish(core, mine, swap(mine), start.T, spectra).T


def solution(mesh):
    raster, slit = mesh.devices.shape
    inner = Mesh(mesh.devices.reshape(raster, slit // 2, 2), ("raster", "z", "core"))
    rows = P(("raster", "z", "core"), None)
    return jax.shard_map(
        functools.partial(body, raster, slit // 2),
        mesh=inner,
        in_specs=(rows, P()),
        out_specs=rows,
        check_vma=False,
    )
```

```python
import functools

import jax
import jax.numpy as jnp
from jax import lax
from jax.experimental import pallas as pl
from jax.experimental.pallas import tpu as pltpu
from jax.sharding import Mesh, PartitionSpec as P

W = 512
K = 64
ITERS = 6
NEAR = (5, 8, 8, 8, 8, 8, 8, 8)
CHUNKS = (256, 768, 1024)
HALF = 3 * 128 + 3 * 64
OFF = (((0, 1), (0, 2), (0, 3)), ((1, 2), (1, 3), (2, 3)))
F32 = jnp.float32
BF16 = jnp.bfloat16
NN = (((1,), (0,)), ((), ()))
NT = (((1,), (1,)), ((), ()))
TN = (((0,), (0,)), ((), ()))


def mul(a, b, dims):
    return lax.dot_general(a, b, dims, preferred_element_type=F32)


def split(value):
    high = value.astype(BF16)
    return high, (value - high.astype(F32)).astype(BF16)


def gram_kernel(core_ref, spectra_ref, keep_ref, send_ref, buf, acc, sems):
    loads = []
    start = 0
    for n, rows in enumerate(CHUNKS):
        at = slice(start, start + rows)
        start += rows
        loads.append((at, pltpu.make_async_copy(spectra_ref.at[at], buf.at[at], sems.at[n])))
        loads[-1][1].start()
    for n, (at, load) in enumerate(loads):
        load.wait()
        high, low = split(buf[at, :])
        h0, h1 = high[:, :256], high[:, 256:]
        l0, l1 = low[:, :256], low[:, 256:]
        sums = (
            0.5 * mul(h0, h0, TN) + mul(h0, l0, TN),
            mul(h0, h1, TN) + mul(h0, l1, TN) + mul(l0, h1, TN),
            0.5 * mul(h1, h1, TN) + mul(h1, l1, TN),
        )
        for block in range(3):
            acc[block] = acc[block] + sums[block] if n else sums[block]

    def block(i, j):
        rows, columns = i % 2 * 128, j % 2 * 128
        return acc[i // 2 + j // 2, rows : rows + 128, columns : columns + 128]

    def put(ref, half):
        for n, (i, j) in enumerate(OFF[half]):
            value = block(i, j)
            if i // 2 == j // 2:
                value = value + block(j, i).T
            ref[n * 128 : n * 128 + 128, :] = value
        right = lax.broadcasted_iota(jnp.int32, (64, 128), 1) >= 64
        corners = []
        for n, i in enumerate((2 * half, 2 * half + 1)):
            value = block(i, i)
            at = 384 + n * 64
            ref[at : at + 64, :] = value[:64] + jnp.where(right, value.T[:64], 0.0)
            corners.append(value[64:])
        ref[512:576, :] = jnp.where(right, corners[1], pltpu.roll(corners[0], 64, 1))

    for core in range(2):

        @pl.when(core_ref[0] == core)
        def _():
            put(keep_ref, core)
            put(send_ref, 1 - core)


def gram_halves(core, spectra):
    rows = spectra.shape[0]
    half = jax.ShapeDtypeStruct((HALF, 128), F32)
    vmem = pl.BlockSpec(memory_space=pltpu.VMEM)
    return pl.pallas_call(
        gram_kernel,
        in_specs=[pl.BlockSpec(memory_space=pltpu.SMEM), pl.BlockSpec(memory_space=pl.ANY)],
        out_specs=[vmem, vmem],
        out_shape=[half, half],
        scratch_shapes=[
            pltpu.VMEM((rows, W), F32),
            pltpu.VMEM((3, 256, 256), F32),
            pltpu.SemaphoreType.DMA((len(CHUNKS),)),
        ],
        compiler_params=pltpu.CompilerParams(vmem_limit_bytes=52 * 1024 * 1024),
    )(core, spectra)


def split_kernel(part, after_ref, spectra_ref, high_ref, low_ref, buf, sems):
    rows = buf.shape[0] // 4
    loads = []
    for n in range(4):
        at = slice(n * rows, n * rows + rows)
        start = part * buf.shape[0] + n * rows
        loads.append((at, pltpu.make_async_copy(spectra_ref.at[start : start + rows], buf.at[at], sems.at[n])))
        loads[-1][1].start()
    for at, load in loads:
        load.wait()
        high_ref[at, :], low_ref[at, :] = split(buf[at, :])


def split_part(part, after, spectra):
    rows = spectra.shape[0] // 2
    anywhere = pl.BlockSpec(memory_space=pl.ANY)
    vmem = pl.BlockSpec(memory_space=pltpu.VMEM)
    half = jax.ShapeDtypeStruct((rows, W), BF16)
    return pl.pallas_call(
        functools.partial(split_kernel, part),
        in_specs=[anywhere, anywhere],
        out_specs=[vmem, vmem],
        out_shape=[half, half],
        scratch_shapes=[pltpu.VMEM((rows, W), F32), pltpu.SemaphoreType.DMA((4,))],
        cost_estimate=pl.CostEstimate(flops=4 * rows * W, bytes_accessed=8 * rows * W, transcendentals=0),
        compiler_params=pltpu.CompilerParams(vmem_limit_bytes=52 * 1024 * 1024),
    )(after, spectra)


def tree(terms):
    while len(terms) > 1:
        terms = [terms[i] + terms[i + 1] if i + 1 < len(terms) else terms[i] for i in range(0, len(terms), 2)]
    return terms[0]


def lanes_of(group, lane):
    return jnp.broadcast_to(group[:, lane : lane + 1], (8, 128))


def row_of(group, i):
    return jnp.broadcast_to(group[i : i + 1, :], (8, 128))


def eliminate(a, one, out_ref):
    sub = lax.broadcasted_iota(jnp.int32, (8, 128), 0)
    square = [one * lanes_of(a[0], 64 + j) for j in range(8)]
    for b in range(8):
        lane = 64 + 8 * b
        panels = {i: [lanes_of(a[i], lane + j) for j in range(8)] for i in range(b + 1, min(b + NEAR[b], 8))}
        following = []
        if b < 7:
            panels[b + 1][0] = one * panels[b + 1][0]
            following = [lanes_of(a[b + 1], lane + 8 + j) for j in range(8)]
        rows = a[b]
        inverse = jnp.zeros((8, 128), F32)
        upper = [jnp.zeros((8, 128), F32)] * 8
        for p in range(0, 8, 2):
            q = p + 1
            first = {c: row_of(square[p], c) for c in range(p, 8)}
            second = {c: row_of(square[q], c) for c in range(q, 8)}
            cofactor = pl.reciprocal(first[p] * second[q] - first[q] * first[q], approx=True)
            invs = (pl.reciprocal(first[p], approx=True), first[p] * cofactor)
            for c in range(q + 1, min(q + 3, 8)):
                left = second[q] * first[c] - first[q] * second[c]
                right = first[p] * second[c] - first[q] * first[c]
                square[c] = square[c] - (square[p] * left + square[q] * right) * cofactor
            downs = [jnp.where(sub > p, square[p], 0.0) * invs[0]]
            square[q] = square[q] - downs[0] * first[q]
            downs.append(jnp.where(sub > q, square[q], 0.0) * invs[1])
            second = {c: row_of(square[q], c) for c in range(q + 1, 8)}
            for c in range(q + 3, 8):
                square[c] = (square[c] - downs[0] * first[c]) - downs[1] * second[c]
            for k, s, inv, down in zip((p, q), (first, second), invs, downs):
                row = row_of(rows, k)
                rows = rows - down * row
                inverse = jnp.where(sub == k, inv, inverse)
                for c in range(k + 1, 8) if b + NEAR[b] < 8 else ():
                    upper[c] = jnp.where(sub == k, s[c], upper[c])
                for i, panel in panels.items():
                    down = panel[k] * inv
                    for c in range(k + 1, 8):
                        panel[c] = panel[c] - down * s[c]
                    if i == b + 1:
                        for c in range(8):
                            following[c] = following[c] - down * row_of(panel[k], c)
                    a[i] = a[i] - down * row
        out_ref[8 * b : 8 * b + 8, :] = rows * (inverse * lax.rsqrt(inverse))
        if b + NEAR[b] < 8:
            q = rows * inverse
            for c in range(7, 0, -1):
                q = q - upper[c] * inverse * row_of(q, c)
            q = [row_of(q, c) for c in range(8)]
            for i in range(b + NEAR[b], 8):
                a[i] = a[i] - tree([lanes_of(a[i], lane + c) * q[c] for c in range(8)])
        square = following


def iterate_kernel(core_ref, mine_ref, other_ref, start_ref, h0_ref, l0_ref, h1_ref, l1_ref, out_ref, gh, gl, basis, rp, sbuf, obuf, sem, osem):
    half = sbuf.shape[1] // 2
    loads = []
    for n, ref in enumerate((h0_ref, l0_ref, h1_ref, l1_ref)):
        at = slice(n // 2 * half, n // 2 * half + half)
        loads.append(pltpu.make_async_copy(ref, sbuf.at[n % 2, at], sem.at[n]))
        loads[-1].start()
    core = core_ref[0]
    zero_is_mine = core == 0

    def put(i, j, value):
        at = (slice(128 * i, 128 * i + 128), slice(128 * j, 128 * j + 128))
        gh[at], gl[at] = split(value)

    right = lax.broadcasted_iota(jnp.int32, (64, 128), 1) >= 64
    for half in range(2):
        first, second = (mine_ref, other_ref) if half == 0 else (other_ref, mine_ref)

        def rows_at(start, count):
            at = slice(start, start + count)
            return jnp.where(zero_is_mine, first[at, :], second[at, :]) * 2.0**-20

        for n, (i, j) in enumerate(OFF[half]):
            value = rows_at(n * 128, 128)
            put(i, j, value)
            put(j, i, value.T)
        corners = rows_at(512, 64)
        for n, i in enumerate((2 * half, 2 * half + 1)):
            corner = jnp.where(right, corners if n else pltpu.roll(corners, 64, 1), 0.0)
            value = jnp.concatenate([rows_at(384 + n * 64, 64), corner], axis=0)
            put(i, i, value + value.T)

    def times_gram(high, low):
        both = mul(jnp.concatenate([high, low], axis=0), gh[...], NN)
        return both[:K] + both[K:] + mul(high, gl[...], NN)

    basis[...] = times_gram(*split(start_ref[...]))
    lanes = lax.broadcasted_iota(jnp.int32, (K, 128), 1)
    eye = (lanes == lax.broadcasted_iota(jnp.int32, (K, 128), 0)).astype(F32)

    one = jnp.where(core >= 0, 1.0, 0.0)

    def step(count, carry):
        image = basis[...]
        ih, il = split(image)
        first = mul(jnp.concatenate([ih, il], axis=0), jnp.concatenate([il, ih], axis=0), NT)
        cross = first[:K] + first[K:] + mul(ih, jnp.concatenate([ih, il], axis=0), NT)
        a = jnp.where(lanes < K, eye, cross)
        wh, wl = split(jnp.where(count == ITERS - 1, image, times_gram(ih, il)))
        eliminate([a[8 * i : 8 * i + 8, :] for i in range(8)], one, rp)
        xh, xl = split(rp[:, :K])
        both = mul(jnp.concatenate([xh, xl], axis=0), wh, NN)
        basis[...] = both[:K] + both[K:] + mul(xh, wl, NN)
        return carry

    lax.fori_loop(0, ITERS, step, 0)
    bh, bl = split(basis[...])
    for load in loads:
        load.wait()
    both = jnp.concatenate([bh, bl], axis=0)
    rows = 512
    stores = []
    for i in range(sbuf.shape[1] // rows):
        at = slice(i * rows, i * rows + rows)
        sh, sl = sbuf[0, at, :], sbuf[1, at, :]
        wide = mul(both, sh, NT)
        obuf[:, at] = wide[:K] + wide[K:] + mul(bh, sl, NT)
        stores.append(pltpu.make_async_copy(obuf.at[:, at], out_ref.at[:, at], osem.at[i]))
        stores[-1].start()
    for store in stores:
        store.wait()


def finish(core, mine, other, start, *parts):
    rows = 2 * parts[0].shape[0]
    vmem = pl.BlockSpec(memory_space=pltpu.VMEM)
    hbm = pl.BlockSpec(memory_space=pl.ANY)
    return pl.pallas_call(
        iterate_kernel,
        in_specs=[pl.BlockSpec(memory_space=pltpu.SMEM), vmem, vmem, vmem, hbm, hbm, hbm, hbm],
        out_specs=hbm,
        out_shape=jax.ShapeDtypeStruct((K, rows), F32),
        scratch_shapes=[
            pltpu.VMEM((W, W), BF16),
            pltpu.VMEM((W, W), BF16),
            pltpu.VMEM((K, W), F32),
            pltpu.VMEM((K, 128), F32),
            pltpu.VMEM((2, rows, W), BF16),
            pltpu.VMEM((K, rows), F32),
            pltpu.SemaphoreType.DMA((4,)),
            pltpu.SemaphoreType.DMA((rows // 512,)),
        ],
        compiler_params=pltpu.CompilerParams(vmem_limit_bytes=52 * 1024 * 1024),
    )(core, mine, other, start, *parts)


def swap(value):
    return lax.ppermute(value, "core", [(0, 1), (1, 0)])


def spread(piece, axis, copies):
    return lax.all_to_all(jnp.broadcast_to(piece[None], (copies, *piece.shape)), axis, 0, 0)


def body(raster, z, spectra, start):
    core = lax.axis_index("core").astype(jnp.int32).reshape(1)
    keep, send = gram_halves(core, spectra)
    arrived = swap(send)
    early = split_part(0, send, spectra)
    arrived, *early = lax.optimization_barrier((arrived, *early))
    part = keep + arrived
    part = lax.all_to_all(part.reshape(raster, 1, HALF * 128 // raster), "raster", 0, 0)
    piece = jnp.sum(part, axis=0)
    piece = jnp.sum(spread(piece, "z", z), axis=0)
    mine = spread(piece, "raster", raster).reshape(HALF, 128)
    other = swap(mine)
    late = split_part(1, mine, spectra)
    return finish(core, mine, other, start.T, *early, *late).T


def solution(mesh):
    raster, slit = mesh.devices.shape
    inner = Mesh(mesh.devices.reshape(raster, slit // 2, 2), ("raster", "z", "core"))
    rows = P(("raster", "z", "core"), None)
    return jax.shard_map(
        functools.partial(body, raster, slit // 2),
        mesh=inner,
        in_specs=(rows, P()),
        out_specs=rows,
        check_vma=False,
    )
```

```python
import functools

import jax
import jax.numpy as jnp
from jax import lax
from jax.experimental import pallas as pl
from jax.experimental.pallas import tpu as pltpu
from jax.sharding import Mesh, PartitionSpec as P

W = 512
K = 64
ITERS = 6
NEAR = (5, 8, 8, 8, 8, 8, 8, 8)
CHUNKS = (256, 768, 1024)
HALF = 3 * 128 + 3 * 64
OFF = (((0, 1), (0, 2), (0, 3)), ((1, 2), (1, 3), (2, 3)))
F32 = jnp.float32
BF16 = jnp.bfloat16
NN = (((1,), (0,)), ((), ()))
NT = (((1,), (1,)), ((), ()))
TN = (((0,), (0,)), ((), ()))


def mul(a, b, dims):
    return lax.dot_general(a, b, dims, preferred_element_type=F32)


def split(value):
    high = value.astype(BF16)
    return high, (value - high.astype(F32)).astype(BF16)


def gram_kernel(core_ref, spectra_ref, keep_ref, send_ref, buf, acc, sems):
    loads = []
    start = 0
    for n, rows in enumerate(CHUNKS):
        at = slice(start, start + rows)
        start += rows
        loads.append((at, pltpu.make_async_copy(spectra_ref.at[at], buf.at[at], sems.at[n])))
        loads[-1][1].start()
    for n, (at, load) in enumerate(loads):
        load.wait()
        high, low = split(buf[at, :])
        h0, h1 = high[:, :256], high[:, 256:]
        l0, l1 = low[:, :256], low[:, 256:]
        sums = (
            0.5 * mul(h0, h0, TN) + mul(h0, l0, TN),
            mul(h0, h1, TN) + mul(h0, l1, TN) + mul(l0, h1, TN),
            0.5 * mul(h1, h1, TN) + mul(h1, l1, TN),
        )
        for block in range(3):
            acc[block] = acc[block] + sums[block] if n else sums[block]

    def block(i, j):
        rows, columns = i % 2 * 128, j % 2 * 128
        return acc[i // 2 + j // 2, rows : rows + 128, columns : columns + 128]

    def put(ref, half):
        for n, (i, j) in enumerate(OFF[half]):
            value = block(i, j)
            if i // 2 == j // 2:
                value = value + block(j, i).T
            ref[n * 128 : n * 128 + 128, :] = value
        right = lax.broadcasted_iota(jnp.int32, (64, 128), 1) >= 64
        corners = []
        for n, i in enumerate((2 * half, 2 * half + 1)):
            value = block(i, i)
            at = 384 + n * 64
            ref[at : at + 64, :] = value[:64] + jnp.where(right, value.T[:64], 0.0)
            corners.append(value[64:])
        ref[512:576, :] = jnp.where(right, corners[1], pltpu.roll(corners[0], 64, 1))

    for core in range(2):

        @pl.when(core_ref[0] == core)
        def _():
            put(keep_ref, core)
            put(send_ref, 1 - core)


def gram_halves(core, spectra):
    rows = spectra.shape[0]
    half = jax.ShapeDtypeStruct((HALF, 128), F32)
    vmem = pl.BlockSpec(memory_space=pltpu.VMEM)
    return pl.pallas_call(
        gram_kernel,
        in_specs=[pl.BlockSpec(memory_space=pltpu.SMEM), pl.BlockSpec(memory_space=pl.ANY)],
        out_specs=[vmem, vmem],
        out_shape=[half, half],
        scratch_shapes=[
            pltpu.VMEM((rows, W), F32),
            pltpu.VMEM((3, 256, 256), F32),
            pltpu.SemaphoreType.DMA((len(CHUNKS),)),
        ],
        compiler_params=pltpu.CompilerParams(vmem_limit_bytes=52 * 1024 * 1024),
    )(core, spectra)


def tree(terms):
    while len(terms) > 1:
        terms = [terms[i] + terms[i + 1] if i + 1 < len(terms) else terms[i] for i in range(0, len(terms), 2)]
    return terms[0]


def lanes_of(group, lane):
    return jnp.broadcast_to(group[:, lane : lane + 1], (8, 128))


def row_of(group, i):
    return jnp.broadcast_to(group[i : i + 1, :], (8, 128))


def eliminate(a, one, out_ref):
    sub = lax.broadcasted_iota(jnp.int32, (8, 128), 0)
    square = [one * lanes_of(a[0], 64 + j) for j in range(8)]
    for b in range(8):
        lane = 64 + 8 * b
        panels = {i: [lanes_of(a[i], lane + j) for j in range(8)] for i in range(b + 1, min(b + NEAR[b], 8))}
        following = []
        if b < 7:
            panels[b + 1][0] = one * panels[b + 1][0]
            following = [lanes_of(a[b + 1], lane + 8 + j) for j in range(8)]
        rows = a[b]
        inverse = jnp.zeros((8, 128), F32)
        upper = [jnp.zeros((8, 128), F32)] * 8
        for p in range(0, 8, 2):
            q = p + 1
            first = {c: row_of(square[p], c) for c in range(p, 8)}
            second = {c: row_of(square[q], c) for c in range(q, 8)}
            cofactor = pl.reciprocal(first[p] * second[q] - first[q] * first[q], approx=True)
            invs = (pl.reciprocal(first[p], approx=True), first[p] * cofactor)
            for c in range(q + 1, min(q + 3, 8)):
                left = second[q] * first[c] - first[q] * second[c]
                right = first[p] * second[c] - first[q] * first[c]
                square[c] = square[c] - (square[p] * left + square[q] * right) * cofactor
            downs = [jnp.where(sub > p, square[p], 0.0) * invs[0]]
            square[q] = square[q] - downs[0] * first[q]
            downs.append(jnp.where(sub > q, square[q], 0.0) * invs[1])
            second = {c: row_of(square[q], c) for c in range(q + 1, 8)}
            for c in range(q + 3, 8):
                square[c] = (square[c] - downs[0] * first[c]) - downs[1] * second[c]
            for k, s, inv, down in zip((p, q), (first, second), invs, downs):
                row = row_of(rows, k)
                rows = rows - down * row
                inverse = jnp.where(sub == k, inv, inverse)
                for c in range(k + 1, 8) if b + NEAR[b] < 8 else ():
                    upper[c] = jnp.where(sub == k, s[c], upper[c])
                for i, panel in panels.items():
                    down = panel[k] * inv
                    for c in range(k + 1, 8):
                        panel[c] = panel[c] - down * s[c]
                    if i == b + 1:
                        for c in range(8):
                            following[c] = following[c] - down * row_of(panel[k], c)
                    a[i] = a[i] - down * row
        out_ref[8 * b : 8 * b + 8, :] = rows * (inverse * lax.rsqrt(inverse))
        if b + NEAR[b] < 8:
            q = rows * inverse
            for c in range(7, 0, -1):
                q = q - upper[c] * inverse * row_of(q, c)
            q = [row_of(q, c) for c in range(8)]
            for i in range(b + NEAR[b], 8):
                a[i] = a[i] - tree([lanes_of(a[i], lane + c) * q[c] for c in range(8)])
        square = following


def iterate_kernel(core_ref, mine_ref, other_ref, start_ref, spectra_ref, out_ref, gh, gl, basis, rp, sbuf, obuf, sem, osem):
    load = pltpu.make_async_copy(spectra_ref, sbuf, sem)
    load.start()
    core = core_ref[0]
    zero_is_mine = core == 0

    def put(i, j, value):
        at = (slice(128 * i, 128 * i + 128), slice(128 * j, 128 * j + 128))
        gh[at], gl[at] = split(value)

    right = lax.broadcasted_iota(jnp.int32, (64, 128), 1) >= 64
    for half in range(2):
        first, second = (mine_ref, other_ref) if half == 0 else (other_ref, mine_ref)

        def rows_at(start, count):
            at = slice(start, start + count)
            return jnp.where(zero_is_mine, first[at, :], second[at, :]) * 2.0**-20

        for n, (i, j) in enumerate(OFF[half]):
            value = rows_at(n * 128, 128)
            put(i, j, value)
            put(j, i, value.T)
        corners = rows_at(512, 64)
        for n, i in enumerate((2 * half, 2 * half + 1)):
            corner = jnp.where(right, corners if n else pltpu.roll(corners, 64, 1), 0.0)
            value = jnp.concatenate([rows_at(384 + n * 64, 64), corner], axis=0)
            put(i, i, value + value.T)

    def times_gram(high, low):
        both = mul(jnp.concatenate([high, low], axis=0), gh[...], NN)
        return both[:K] + both[K:] + mul(high, gl[...], NN)

    basis[...] = times_gram(*split(start_ref[...]))
    lanes = lax.broadcasted_iota(jnp.int32, (K, 128), 1)
    eye = (lanes == lax.broadcasted_iota(jnp.int32, (K, 128), 0)).astype(F32)

    one = jnp.where(core >= 0, 1.0, 0.0)

    def step(count, carry):
        image = basis[...]
        ih, il = split(image)
        first = mul(jnp.concatenate([ih, il], axis=0), jnp.concatenate([il, ih], axis=0), NT)
        cross = first[:K] + first[K:] + mul(ih, jnp.concatenate([ih, il], axis=0), NT)
        a = jnp.where(lanes < K, eye, cross)
        wh, wl = split(jnp.where(count == ITERS - 1, image, times_gram(ih, il)))
        eliminate([a[8 * i : 8 * i + 8, :] for i in range(8)], one, rp)
        xh, xl = split(rp[:, :K])
        both = mul(jnp.concatenate([xh, xl], axis=0), wh, NN)
        basis[...] = both[:K] + both[K:] + mul(xh, wl, NN)
        return carry

    lax.fori_loop(0, ITERS, step, 0)
    bh, bl = split(basis[...])
    load.wait()
    both = jnp.concatenate([bh, bl], axis=0)
    rows = 256
    stores = []
    for i in range(sbuf.shape[0] // rows):
        at = slice(i * rows, i * rows + rows)
        sh, sl = split(sbuf[at, :])
        wide = mul(both, sh, NT)
        obuf[:, at] = wide[:K] + wide[K:] + mul(bh, sl, NT)
        stores.append(pltpu.make_async_copy(obuf.at[:, at], out_ref.at[:, at], osem.at[i]))
        stores[-1].start()
    for store in stores:
        store.wait()


def finish(core, mine, other, start, spectra):
    rows = spectra.shape[0]
    vmem = pl.BlockSpec(memory_space=pltpu.VMEM)
    hbm = pl.BlockSpec(memory_space=pl.ANY)
    return pl.pallas_call(
        iterate_kernel,
        in_specs=[pl.BlockSpec(memory_space=pltpu.SMEM), vmem, vmem, vmem, hbm],
        out_specs=hbm,
        out_shape=jax.ShapeDtypeStruct((K, rows), F32),
        scratch_shapes=[
            pltpu.VMEM((W, W), BF16),
            pltpu.VMEM((W, W), BF16),
            pltpu.VMEM((K, W), F32),
            pltpu.VMEM((K, 128), F32),
            pltpu.VMEM((rows, W), F32),
            pltpu.VMEM((K, rows), F32),
            pltpu.SemaphoreType.DMA,
            pltpu.SemaphoreType.DMA((rows // 256,)),
        ],
        compiler_params=pltpu.CompilerParams(vmem_limit_bytes=52 * 1024 * 1024),
    )(core, mine, other, start, spectra)


def swap(value):
    return lax.ppermute(value, "core", [(0, 1), (1, 0)])


def spread(piece, axis, copies):
    return lax.all_to_all(jnp.broadcast_to(piece[None], (copies, *piece.shape)), axis, 0, 0)


def body(raster, z, spectra, start):
    core = lax.axis_index("core").astype(jnp.int32).reshape(1)
    keep, send = gram_halves(core, spectra)
    part = keep + swap(send)
    part = lax.all_to_all(part.reshape(raster, 1, HALF * 128 // raster), "raster", 0, 0)
    piece = jnp.sum(part, axis=0)
    piece = jnp.sum(spread(piece, "z", z), axis=0)
    mine = spread(piece, "raster", raster).reshape(HALF, 128)
    return finish(core, mine, swap(mine), start.T, spectra).T


def solution(mesh):
    raster, slit = mesh.devices.shape
    inner = Mesh(mesh.devices.reshape(raster, slit // 2, 2), ("raster", "z", "core"))
    rows = P(("raster", "z", "core"), None)
    return jax.shard_map(
        functools.partial(body, raster, slit // 2),
        mesh=inner,
        in_specs=(rows, P()),
        out_specs=rows,
        check_vma=False,
    )
```
